32 devices in a mesh: ka: 2 (over core), ga: 16 (over z, y, x).
Axes of the slice: x: 2, y: 2, z: 4, core: 2. Of those that a mesh axis runs over, the one named last changes fastest.
Arguments:
- wavefunctions: bfloat16 [16, 2, 16, 32, 256], P('ka', None, None, 'ga'), may hold values from -6 to 6
- partner: int32 [16], replicated, may hold values from 0 to 15, each once
- gmap: int32 [8192], replicated, may hold values from 0 to 8191, as said below
- screened: bfloat16 [8192, 8192], P('ga'), may hold values from -0.0007324219 to 0.0007324219
Outputs:
- kernel_rows: float32 [16, 2, 4096], P('ka')
- kernel_mirror: float32 [16, 2, 4096], P('ka')
The draws below stay inside these ranges and needn't reach their ends.
Inputs may be any that keep to these rules, and one draw needn't show every extreme that they name: `partner`: each k-point appears exactly once. Entries j and gmap[j] lie in the same aligned block of 32; within each block every index appears once.
All inputs are finite; a program needn't handle non-finite values.
Results may differ from the reference program's by a relative error of at most 0.0042.
Values may be sent and summed in bfloat16 or wider, within the bound.
A program may use at most 256 MiB of HBM per device.

```python
import jax
import jax.numpy as jnp
from jax import lax

NV = 8
NC = 8
NX = 16
NY = 16
NZ = 32
NB = 16
NXY = 256
NG = 8192
NF = 128
NK = 16


def draw_gmap(key, part):
    key = jax.random.fold_in(key, 11)
    column_keys = jax.random.split(key, NX * NY)
    shuffled = jax.vmap(lambda column_key: jax.random.permutation(column_key, NZ))(column_keys)
    offsets = NZ * jnp.arange(NX * NY, dtype=jnp.int32)[:, None]
    return (shuffled.astype(jnp.int32) + offsets).reshape(NX * NY * NZ).astype(jnp.int32)


def shard_levels(own_key, extent, cuts, smallest, high):
    factor_of = 1.0
    for dim, shards_of in cuts:
        steps = jax.random.uniform(jax.random.fold_in(jax.random.fold_in(own_key, 6), dim), (shards_of,), jnp.float32, smallest / len(cuts), high / len(cuts))
        factor_of = factor_of * jnp.repeat(jnp.exp(steps), extent[dim] // shards_of).reshape((-1,) + (1,) * (len(extent) - 1 - dim))
    return factor_of


def bell_draw(own_key, extent, width, most, shards=(), kind=jnp.bfloat16):
    values = jax.random.normal(own_key, extent, jnp.float32) * width
    if len(shards) > 0:
        values = shard_levels(own_key, extent, shards, -0.22, 0.18) * values
    return jnp.clip(values, min=-most, max=most).astype(kind)


def setup_inputs(seed: int = 0) -> dict:
    key_of = jax.random.split(jax.random.key(seed), 5)
    return {
        "wavefunctions": bell_draw(key_of[0], (NK, 2, NB, NZ, NXY), 1.0, 6.0, ((0, 2), (3, 16))),
        "partner": jax.random.permutation(key_of[1], NK).astype(jnp.int32),
        "gmap": draw_gmap(jax.random.fold_in(key_of[4], 71), 0),
        "screened": bell_draw(key_of[3], (NG, NG), (NG * NG) ** -0.5, 0.0007324219, ((0, 16),)),
    }


def pair_density(left, right):
    product = jnp.conj(left[:, :, None]) * right[:, None, :]
    return product.reshape(left.shape[0], left.shape[1] * right.shape[1], NX, NY, NZ)

def swap_blocks(blocks):
    count = blocks.shape[0]
    moved = blocks.reshape(count, 2, NC, NC, NV, NV).transpose(0, 1, 3, 2, 5, 4).reshape(count, 2, NC * NC * NV * NV)
    return moved * jnp.array([1.0, -1.0], dtype=jnp.float32)[None, :, None]

def reference(wavefunctions, partner, gmap, screened):
    values = wavefunctions.astype(jnp.float32)
    waves = values[:, 0] + 1j * values[:, 1]
    waves = waves.reshape(NK, NB, NZ, NX, NY).transpose(0, 1, 3, 4, 2)
    home = waves
    away = waves[partner]
    cond_rho = pair_density(home[:, NV:], away[:, NV:])
    val_rho = pair_density(home[:, :NV], away[:, :NV])
    density = jnp.concatenate([cond_rho, val_rho], axis=1)
    spectrum = jnp.fft.fftn(density, axes=(-3, -2, -1)) / jnp.sqrt(jnp.float32(NG))
    spectrum = spectrum.reshape(NK, NF, NG)
    parts = jnp.stack([jnp.real(spectrum).astype(jnp.bfloat16), jnp.imag(spectrum).astype(jnp.bfloat16)], axis=1)
    ordered = parts[:, :, :, gmap]
    cond_part = ordered[:, :, :NC * NC, :]
    val_part = ordered[:, :, NC * NC:, :]
    val_cols = val_part.transpose(3, 0, 1, 2).reshape(NG, NK * 2 * NV * NV)
    response = jnp.dot(screened.astype(jnp.float32), val_cols.astype(jnp.float32), precision=lax.Precision.HIGHEST)
    response = response.reshape(NG, NK, 2, NV * NV)
    cond_f = cond_part.astype(jnp.float32).transpose(3, 0, 1, 2)
    highest = lax.Precision.HIGHEST
    real_out = jnp.einsum('gkc,gkv->kcv', cond_f[:, :, 0], response[:, :, 0], precision=highest) + jnp.einsum('gkc,gkv->kcv', cond_f[:, :, 1], response[:, :, 1], precision=highest)
    imag_out = jnp.einsum('gkc,gkv->kcv', cond_f[:, :, 0], response[:, :, 1], precision=highest) - jnp.einsum('gkc,gkv->kcv', cond_f[:, :, 1], response[:, :, 0], precision=highest)
    kernel = jnp.stack([real_out, imag_out], axis=1).reshape(NK, 2, NC * NC * NV * NV)
    kernel_rows = kernel
    kernel_mirror = jnp.zeros_like(kernel).at[partner].set(swap_blocks(kernel))
    return (kernel_rows, kernel_mirror)
```

```python
import functools
import math

import jax
import jax.numpy as jnp
import numpy as np
from jax import lax
from jax.experimental import pallas as pl
from jax.experimental.pallas import tpu as pltpu
from jax.sharding import PartitionSpec as P

NV = 8
NC = 8
NX = 16
NY = 16
NZ = 32
NXY = NX * NY
NG = NXY * NZ
PAIRS = 64
GROUP = 256
STEP_Z = 8
BF = jnp.bfloat16
F32 = jnp.float32
VMEM_LIMIT = 56 * 1024 * 1024
SCALE_16 = 1.1329
SCALE_32 = 1.6245


def split(values):
    high = values.astype(BF)
    return high, (values - high.astype(F32)).astype(BF)


def line_table():
    z = np.arange(NZ)
    angle = -2.0 * np.pi * (z[:, None] * z[None, :] % NZ) / NZ
    return SCALE_32 * np.concatenate([np.cos(angle), np.sin(angle)], axis=0)


def plane_table():
    r = np.arange(NXY)
    x, y = r // NY, r % NY
    turns = (x[:, None] * x[None, :] % NX) / NX + (y[:, None] * y[None, :] % NY) / NY
    c, s = np.cos(-2.0 * np.pi * turns), np.sin(-2.0 * np.pi * turns)
    return SCALE_16 * np.block([[c, -s], [s, c]])


def interaction_kernel(steps, line_ref, plane_ref, gz_ref, w_ref, out_ref, mid_ref, low_ref):
    step = pl.program_id(0)
    rows = w_ref.shape[0]
    per = w_ref.shape[1] // GROUP
    cols = GROUP // NZ

    @pl.when(step < steps)
    def _():
        parts = []
        for g in range(per):
            gz = gz_ref[0, :, g * GROUP : (g + 1) * GROUP]
            hot = lax.broadcasted_iota(jnp.int32, (NZ, GROUP), 0) == gz
            table = jnp.dot(line_ref[...], hot.astype(F32).astype(BF), preferred_element_type=F32)
            column = lax.broadcasted_iota(jnp.int32, (cols, GROUP), 1) // NZ
            mask = column == lax.broadcasted_iota(jnp.int32, (cols, GROUP), 0)
            wide = jnp.where(mask[None], table[:, None, :], 0.0)
            wide = wide.reshape(2 * NZ * cols, GROUP).astype(BF)
            got = lax.dot_general(
                wide,
                w_ref[:, g * GROUP : (g + 1) * GROUP],
                (((1,), (1,)), ((), ())),
                preferred_element_type=F32,
            )
            parts.append(got.reshape(2, NZ, cols, rows))
        high, low = split(jnp.concatenate(parts, axis=2))
        start = pl.multiple_of(step * (per * cols), per * cols)
        for p in range(2):
            mid_ref[:, p, pl.ds(start, per * cols), :] = high[p]
            low_ref[:, p, pl.ds(start, per * cols), :] = low[p]

    @pl.when(step >= steps)
    def _():
        planes = out_ref.shape[0]
        for i in range(planes):
            z = (step - steps) * planes + i
            mid = mid_ref[z].reshape(2 * NXY, rows)
            low = low_ref[z].reshape(2 * NXY, rows)
            got = jnp.dot(plane_ref[...], mid, preferred_element_type=F32)
            got = (got + jnp.dot(plane_ref[...], low, preferred_element_type=F32)).astype(BF)
            out_ref[i, :, :rows] = got[:NXY]
            out_ref[i, :, rows:] = got[NXY:]


def transformed_interaction(gmap, screened):
    rows = screened.shape[0]
    per = 2
    steps = NG // (GROUP * per)
    planes = 2
    gz = (gmap % NZ).reshape(steps, 1, GROUP * per)
    last = steps - 1
    return pl.pallas_call(
        functools.partial(interaction_kernel, steps),
        grid=(steps + NZ // planes,),
        in_specs=[
            pl.BlockSpec((2 * NZ, NZ), lambda i: (0, 0)),
            pl.BlockSpec((2 * NXY, 2 * NXY), lambda i: (0, 0)),
            pl.BlockSpec((1, 1, GROUP * per), lambda i: (jnp.minimum(i, last), 0, 0)),
            pl.BlockSpec((rows, GROUP * per), lambda i: (0, jnp.minimum(i, last))),
        ],
        out_specs=pl.BlockSpec(
            (planes, NXY, 2 * rows), lambda i: (jnp.maximum(i - steps, 0), 0, 0)
        ),
        out_shape=jax.ShapeDtypeStruct((NZ, NXY, 2 * rows), BF),
        scratch_shapes=[pltpu.VMEM((NZ, 2, NXY, rows), BF)] * 2,
        compiler_params=pltpu.CompilerParams(vmem_limit_bytes=VMEM_LIMIT),
        cost_estimate=pl.CostEstimate(
            flops=16 * NXY * NG * rows, bytes_accessed=6 * NG * rows, transcendentals=0
        ),
    )(jnp.asarray(line_table(), BF), jnp.asarray(plane_table(), BF), gz, screened)


def pair_rows(left, right):
    left_real, left_imag = left
    right_real, right_imag = right
    real_part = [
        left_real[b : b + 1] * right_real + left_imag[b : b + 1] * right_imag for b in range(8)
    ]
    imag_part = [
        left_real[b : b + 1] * right_imag - left_imag[b : b + 1] * right_real for b in range(8)
    ]
    return (
        jnp.concatenate(real_part, axis=0),
        jnp.concatenate(imag_part, axis=0),
    )


def contraction_kernel(
    pairs,
    who_ref,
    waves_ref,
    inter_ref,
    first_ref,
    second_ref,
    out_ref,
    val_ref,
    cond_ref,
    cond_low_ref,
    response_ref,
    spectrum_ref,
):
    step = pl.program_id(0)
    half = pairs * PAIRS
    rows = response_ref.shape[1] // 2

    def fill(k, carry):
        for z in range(STEP_Z):
            home = waves_ref[who_ref[0], z, k].astype(F32)
            away = waves_ref[who_ref[1 + k], z, who_ref[1 + pairs + k]].astype(F32)
            for first in (0, NV):
                left = (home[0, first : first + 8], home[1, first : first + 8])
                right = (away[0, first : first + 8], away[1, first : first + 8])
                real_part, imag_part = pair_rows(left, right)
                start = pl.multiple_of(k * PAIRS, PAIRS)
                lanes = slice(z * NXY, (z + 1) * NXY)
                if first == 0:
                    val_ref[pl.ds(start, PAIRS), lanes] = real_part.astype(BF)
                    val_ref[pl.ds(half + start, PAIRS), lanes] = imag_part.astype(BF)
                else:
                    high, low = split(real_part)
                    cond_ref[pl.ds(start, PAIRS), lanes] = high
                    cond_low_ref[pl.ds(start, PAIRS), lanes] = low
                    high, low = split(imag_part)
                    cond_ref[pl.ds(half + start, PAIRS), lanes] = high
                    cond_low_ref[pl.ds(half + start, PAIRS), lanes] = low
        return carry

    lax.fori_loop(0, pairs, fill, 0)

    @pl.when(step == 0)
    def _():
        response_ref[...] = jnp.zeros_like(response_ref)
        spectrum_ref[...] = jnp.zeros_like(spectrum_ref)

    inter = inter_ref[...].reshape(STEP_Z * NXY, 2 * rows)
    response_ref[...] += jnp.dot(val_ref[...], inter, preferred_element_type=F32)
    mixed = jnp.dot(cond_ref[...], first_ref[...], preferred_element_type=F32)
    mixed = mixed + jnp.dot(cond_low_ref[...], first_ref[...], preferred_element_type=F32)
    mixed, mixed_low = split(mixed)
    spectrum_ref[...] += jnp.dot(mixed, second_ref[0], preferred_element_type=F32) + jnp.dot(
        mixed_low, second_ref[0], preferred_element_type=F32
    )

    @pl.when(step == pl.num_programs(0) - 1)
    def _():
        def finish(k, carry):
            start = pl.multiple_of(k * PAIRS, PAIRS)
            top = pl.ds(start, PAIRS)
            low = pl.ds(half + start, PAIRS)

            def whole(ref):
                real_part = ref[top, :rows] - ref[low, rows:]
                imag_part = ref[top, rows:] + ref[low, :rows]
                return split(jnp.concatenate([real_part, imag_part], axis=0))

            def mixed_product(left, right):
                return lax.dot_general(
                    left, right, (((1,), (1,)), ((), ())), preferred_element_type=F32
                )

            cond, cond_low = whole(spectrum_ref)
            resp, resp_low = whole(response_ref)
            product = mixed_product(cond, resp)
            product = product + mixed_product(cond_low, resp) + mixed_product(cond, resp_low)
            scale = 1.0 / (NG * (SCALE_16 * SCALE_32) ** 2)
            a, b = product[:PAIRS], product[PAIRS:]
            out_ref[k, 0] = (a[:, :PAIRS] + b[:, PAIRS:]) * scale
            out_ref[k, 1] = (a[:, PAIRS:] - b[:, :PAIRS]) * scale
            return carry

        lax.fori_loop(0, pairs, finish, 0)


def partial_kernel(who, waves, inter, first, second):
    holders, _, pairs = waves.shape[:3]
    rows2 = inter.shape[2]
    half2 = 2 * pairs * PAIRS
    steps = NZ // STEP_Z
    spec = pltpu.PrefetchScalarGridSpec(
        num_scalar_prefetch=1,
        grid=(steps,),
        in_specs=[
            pl.BlockSpec(
                (holders, STEP_Z, pairs, 2, NV + NC, NXY), lambda i, who: (0, i, 0, 0, 0, 0)
            ),
            pl.BlockSpec((STEP_Z, NXY, rows2), lambda i, who: (i, 0, 0)),
            pl.BlockSpec(first.shape, lambda i, who: (0, 0)),
            pl.BlockSpec((1,) + second.shape[1:], lambda i, who: (i, 0, 0)),
        ],
        out_specs=pl.BlockSpec((pairs, 2, PAIRS, PAIRS), lambda i, who: (0, 0, 0, 0)),
        scratch_shapes=[
            pltpu.VMEM((half2, STEP_Z * NXY), BF),
            pltpu.VMEM((half2, STEP_Z * NXY), BF),
            pltpu.VMEM((half2, STEP_Z * NXY), BF),
            pltpu.VMEM((half2, rows2), F32),
            pltpu.VMEM((half2, rows2), F32),
        ],
    )
    return pl.pallas_call(
        functools.partial(contraction_kernel, pairs),
        grid_spec=spec,
        out_shape=jax.ShapeDtypeStruct((pairs, 2, PAIRS, PAIRS), F32),
        compiler_params=pltpu.CompilerParams(vmem_limit_bytes=VMEM_LIMIT),
        cost_estimate=pl.CostEstimate(
            flops=2 * half2 * rows2 * NG, bytes_accessed=2 * inter.size, transcendentals=0
        ),
    )(who, waves, inter, first, second)


def local_tables(gmap, place, rows):
    columns = rows // NZ
    number = place * columns + jnp.arange(columns, dtype=jnp.int32)
    gx, gy = number // NY, number % NY
    r = jnp.arange(NXY, dtype=jnp.int32)
    turns = ((r // NY)[:, None] * gx[None] + (r % NY)[:, None] * gy[None]) % NX
    angle = turns.astype(F32) * (-2.0 * math.pi / NX)
    plane = SCALE_16 * jnp.stack([jnp.cos(angle), jnp.sin(angle)], axis=1)
    same = jnp.asarray(np.eye(STEP_Z), F32)
    first = same[:, None, :, None, None] * plane[None, :, None]
    first = first.reshape(STEP_Z * NXY, STEP_Z * 2 * columns).astype(BF)
    gz = lax.dynamic_slice_in_dim(gmap, place * rows, rows) % NZ
    z = jnp.arange(NZ, dtype=jnp.int32)
    angle = (z[:, None] * gz[None] % NZ).astype(F32) * (-2.0 * math.pi / NZ)
    c, s = SCALE_32 * jnp.cos(angle), SCALE_32 * jnp.sin(angle)
    line = jnp.stack([jnp.stack([c, s], axis=1), jnp.stack([-s, c], axis=1)], axis=1)
    own = (jnp.arange(rows) // NZ)[None, :] == jnp.arange(columns)[:, None]
    second = jnp.where(own[None, None, :, None, :], line[:, :, None], 0.0)
    second = second.reshape(NZ // STEP_Z, STEP_Z * 2 * columns, 2 * rows).astype(BF)
    return first, second


def swap_blocks(blocks):
    number = blocks.shape[0]
    moved = (
        blocks.reshape(number, 2, NC, NC, NV, NV)
        .transpose(0, 1, 3, 2, 5, 4)
        .reshape(number, 2, NC * NC * NV * NV)
    )
    return moved * jnp.array([1.0, -1.0], dtype=F32)[None, :, None]


def on_device(wavefunctions, partner, gmap, screened):
    pairs = wavefunctions.shape[0]
    ka_place = lax.axis_index("ka")
    ga_place = lax.axis_index("ga")
    owned = ka_place * pairs + jnp.arange(pairs, dtype=jnp.int32)
    wanted = partner[owned]
    waves = lax.all_gather(wavefunctions.transpose(3, 0, 1, 2, 4), "ga", axis=0, tiled=True)
    waves = lax.all_gather(waves, "ka", axis=0)
    inter = transformed_interaction(gmap, screened)
    first, second = local_tables(gmap, ga_place, screened.shape[0])
    who = jnp.concatenate([ka_place[None].astype(jnp.int32), wanted // pairs, wanted % pairs])
    part = partial_kernel(who, waves, inter, first, second)
    summed = lax.psum(part.reshape(pairs, 2, NC * NC * NV * NV), "ga")
    everyone = lax.all_gather(summed, "ka", axis=0, tiled=True)
    source = jnp.sum(
        jnp.where(
            partner[None, :] == owned[:, None],
            jnp.arange(partner.shape[0], dtype=jnp.int32)[None],
            0,
        ),
        axis=1,
    )
    mirror_out = swap_blocks(jnp.take(everyone, source, axis=0))
    return (summed, mirror_out)


def solution(mesh):
    in_specs = (P("ka", None, None, "ga", None), P(), P(), P("ga", None))
    out_specs = (P("ka", None, None), P("ka", None, None))
    return jax.shard_map(
        on_device, mesh=mesh, in_specs=in_specs, out_specs=out_specs, check_vma=False
    )
```

```python
import functools
import math

import jax
import jax.numpy as jnp
import numpy as np
from jax import lax
from jax.experimental import pallas as pl
from jax.experimental.pallas import tpu as pltpu
from jax.sharding import PartitionSpec as P

NV = 8
NC = 8
NX = 16
NY = 16
NZ = 32
NXY = NX * NY
NG = NXY * NZ
PAIRS = 64
GROUP = 256
STEP_Z = 8
BF = jnp.bfloat16
F32 = jnp.float32
VMEM_LIMIT = 56 * 1024 * 1024
SCALE_16 = 1.1329
SCALE_32 = 1.6245


def split(values):
    high = values.astype(BF)
    return high, (values - high.astype(F32)).astype(BF)


def line_table():
    z = np.arange(NZ)
    angle = -2.0 * np.pi * (z[:, None] * z[None, :] % NZ) / NZ
    return SCALE_32 * np.concatenate([np.cos(angle), np.sin(angle)], axis=0)


def plane_table():
    r = np.arange(NXY)
    x, y = r // NY, r % NY
    turns = (x[:, None] * x[None, :] % NX) / NX + (y[:, None] * y[None, :] % NY) / NY
    c, s = np.cos(-2.0 * np.pi * turns), np.sin(-2.0 * np.pi * turns)
    return SCALE_16 * np.block([[c, -s], [s, c]])


def interaction_kernel(steps, line_ref, plane_ref, gz_ref, w_ref, out_ref, mid_ref, low_ref):
    step = pl.program_id(0)
    rows = w_ref.shape[0]
    per = w_ref.shape[1] // GROUP
    cols = GROUP // NZ

    @pl.when(step < steps)
    def _():
        parts = []
        for g in range(per):
            gz = gz_ref[0, :, g * GROUP : (g + 1) * GROUP]
            hot = lax.broadcasted_iota(jnp.int32, (NZ, GROUP), 0) == gz
            table = jnp.dot(line_ref[...], hot.astype(F32).astype(BF), preferred_element_type=F32)
            column = lax.broadcasted_iota(jnp.int32, (cols, GROUP), 1) // NZ
            mask = column == lax.broadcasted_iota(jnp.int32, (cols, GROUP), 0)
            wide = jnp.where(mask[None], table[:, None, :], 0.0)
            wide = wide.reshape(2 * NZ * cols, GROUP).astype(BF)
            got = lax.dot_general(
                wide,
                w_ref[:, g * GROUP : (g + 1) * GROUP],
                (((1,), (1,)), ((), ())),
                preferred_element_type=F32,
            )
            parts.append(got.reshape(2, NZ, cols, rows))
        high, low = split(jnp.concatenate(parts, axis=2))
        start = pl.multiple_of(step * (per * cols), per * cols)
        for p in range(2):
            mid_ref[:, p, pl.ds(start, per * cols), :] = high[p]
            low_ref[:, p, pl.ds(start, per * cols), :] = low[p]

    @pl.when(step >= steps)
    def _():
        planes = out_ref.shape[0]
        for i in range(planes):
            z = (step - steps) * planes + i
            mid = mid_ref[z].reshape(2 * NXY, rows)
            low = low_ref[z].reshape(2 * NXY, rows)
            got = jnp.dot(plane_ref[...], mid, preferred_element_type=F32)
            got = (got + jnp.dot(plane_ref[...], low, preferred_element_type=F32)).astype(BF)
            out_ref[i, :, :rows] = got[:NXY]
            out_ref[i, :, rows:] = got[NXY:]


def transformed_interaction(gmap, screened):
    rows = screened.shape[0]
    per = 2
    steps = NG // (GROUP * per)
    planes = 2
    gz = (gmap % NZ).reshape(steps, 1, GROUP * per)
    last = steps - 1
    return pl.pallas_call(
        functools.partial(interaction_kernel, steps),
        grid=(steps + NZ // planes,),
        in_specs=[
            pl.BlockSpec((2 * NZ, NZ), lambda i: (0, 0)),
            pl.BlockSpec((2 * NXY, 2 * NXY), lambda i: (0, 0)),
            pl.BlockSpec((1, 1, GROUP * per), lambda i: (jnp.minimum(i, last), 0, 0)),
            pl.BlockSpec((rows, GROUP * per), lambda i: (0, jnp.minimum(i, last))),
        ],
        out_specs=pl.BlockSpec(
            (planes, NXY, 2 * rows), lambda i: (jnp.maximum(i - steps, 0), 0, 0)
        ),
        out_shape=jax.ShapeDtypeStruct((NZ, NXY, 2 * rows), BF),
        scratch_shapes=[pltpu.VMEM((NZ, 2, NXY, rows), BF)] * 2,
        compiler_params=pltpu.CompilerParams(vmem_limit_bytes=VMEM_LIMIT),
        cost_estimate=pl.CostEstimate(
            flops=16 * NXY * NG * rows, bytes_accessed=6 * NG * rows, transcendentals=0
        ),
    )(jnp.asarray(line_table(), BF), jnp.asarray(plane_table(), BF), gz, screened)


def pair_rows(left, right):
    left_real, left_imag = left
    right_real, right_imag = right
    real_part = [
        left_real[b : b + 1] * right_real + left_imag[b : b + 1] * right_imag for b in range(8)
    ]
    imag_part = [
        left_real[b : b + 1] * right_imag - left_imag[b : b + 1] * right_real for b in range(8)
    ]
    return (
        jnp.concatenate(real_part, axis=0),
        jnp.concatenate(imag_part, axis=0),
    )


def fill_planes(who_ref, waves_ref, pairs, store):
    def fill(k, carry):
        for z in range(STEP_Z):
            home = waves_ref[who_ref[0], z, k].astype(F32)
            away = waves_ref[who_ref[1 + k], z, who_ref[1 + pairs + k]].astype(F32)
            real_part, imag_part = pair_rows((home[:8], home[8:]), (away[:8], away[8:]))
            lanes = slice(z * NXY, (z + 1) * NXY)
            start = pl.multiple_of(k * PAIRS, PAIRS)
            store(pl.ds(start, PAIRS), lanes, real_part)
            store(pl.ds(pairs * PAIRS + start, PAIRS), lanes, imag_part)
        return carry

    lax.fori_loop(0, pairs, fill, 0)


def response_kernel(pairs, who_ref, waves_ref, inter_ref, out_ref, val_ref):
    def store(rows, lanes, values):
        val_ref[rows, lanes] = values.astype(BF)

    fill_planes(who_ref, waves_ref, pairs, store)

    @pl.when(pl.program_id(0) == 0)
    def _():
        out_ref[...] = jnp.zeros_like(out_ref)

    inter = inter_ref[...].reshape(STEP_Z * NXY, inter_ref.shape[2])
    out_ref[...] += jnp.dot(val_ref[...], inter, preferred_element_type=F32)


def block_kernel(
    pairs,
    who_ref,
    waves_ref,
    response_ref,
    first_ref,
    second_ref,
    out_ref,
    cond_ref,
    cond_low_ref,
    spectrum_ref,
):
    step = pl.program_id(0)
    half = pairs * PAIRS
    rows = response_ref.shape[1] // 2

    def store(where, lanes, values):
        high, low = split(values)
        cond_ref[where, lanes] = high
        cond_low_ref[where, lanes] = low

    fill_planes(who_ref, waves_ref, pairs, store)

    @pl.when(step == 0)
    def _():
        spectrum_ref[...] = jnp.zeros_like(spectrum_ref)

    mixed = jnp.dot(cond_ref[...], first_ref[...], preferred_element_type=F32)
    mixed = mixed + jnp.dot(cond_low_ref[...], first_ref[...], preferred_element_type=F32)
    mixed, mixed_low = split(mixed)
    spectrum_ref[...] += jnp.dot(mixed, second_ref[0], preferred_element_type=F32) + jnp.dot(
        mixed_low, second_ref[0], preferred_element_type=F32
    )

    @pl.when(step == pl.num_programs(0) - 1)
    def _():
        def finish(k, carry):
            start = pl.multiple_of(k * PAIRS, PAIRS)
            top = pl.ds(start, PAIRS)
            low = pl.ds(half + start, PAIRS)

            def whole(ref):
                real_part = ref[top, :rows] - ref[low, rows:]
                imag_part = ref[top, rows:] + ref[low, :rows]
                return split(jnp.concatenate([real_part, imag_part], axis=0))

            def mixed_product(left, right):
                return lax.dot_general(
                    left, right, (((1,), (1,)), ((), ())), preferred_element_type=F32
                )

            cond, cond_low = whole(spectrum_ref)
            resp, resp_low = whole(response_ref)
            product = mixed_product(cond, resp)
            product = product + mixed_product(cond_low, resp) + mixed_product(cond, resp_low)
            scale = 1.0 / (NG * (SCALE_16 * SCALE_32) ** 2)
            a, b = product[:PAIRS], product[PAIRS:]
            real_part = a[:, :PAIRS] + b[:, PAIRS:]
            imag_part = a[:, PAIRS:] - b[:, :PAIRS]
            out_ref[top, :] = jnp.concatenate([real_part, imag_part], axis=1) * scale
            return carry

        lax.fori_loop(0, pairs, finish, 0)


def waves_spec(waves):
    shape = (waves.shape[0], STEP_Z) + waves.shape[2:]
    return pl.BlockSpec(shape, lambda i, who: (0, i, 0, 0, 0))


def all_responses(who, waves, inter):
    pairs = waves.shape[2]
    rows2 = inter.shape[2]
    half2 = 2 * pairs * PAIRS
    spec = pltpu.PrefetchScalarGridSpec(
        num_scalar_prefetch=1,
        grid=(NZ // STEP_Z,),
        in_specs=[
            waves_spec(waves),
            pl.BlockSpec((STEP_Z, NXY, rows2), lambda i, who: (i, 0, 0)),
        ],
        out_specs=pl.BlockSpec((half2, rows2), lambda i, who: (0, 0)),
        scratch_shapes=[pltpu.VMEM((half2, STEP_Z * NXY), BF)],
    )
    return pl.pallas_call(
        functools.partial(response_kernel, pairs),
        grid_spec=spec,
        out_shape=jax.ShapeDtypeStruct((half2, rows2), F32),
        compiler_params=pltpu.CompilerParams(vmem_limit_bytes=VMEM_LIMIT),
        cost_estimate=pl.CostEstimate(
            flops=2 * half2 * rows2 * NG, bytes_accessed=2 * inter.size, transcendentals=0
        ),
    )(who, waves, inter)


def partial_blocks(who, waves, response, first, second):
    pairs = waves.shape[2]
    half2, rows2 = response.shape
    spec = pltpu.PrefetchScalarGridSpec(
        num_scalar_prefetch=1,
        grid=(NZ // STEP_Z,),
        in_specs=[
            waves_spec(waves),
            pl.BlockSpec((half2, rows2), lambda i, who: (0, 0)),
            pl.BlockSpec(first.shape, lambda i, who: (0, 0)),
            pl.BlockSpec((1,) + second.shape[1:], lambda i, who: (i, 0, 0)),
        ],
        out_specs=pl.BlockSpec((pairs * PAIRS, 2 * PAIRS), lambda i, who: (0, 0)),
        scratch_shapes=[
            pltpu.VMEM((half2, STEP_Z * NXY), BF),
            pltpu.VMEM((half2, STEP_Z * NXY), BF),
            pltpu.VMEM((half2, rows2), F32),
        ],
    )
    return pl.pallas_call(
        functools.partial(block_kernel, pairs),
        grid_spec=spec,
        out_shape=jax.ShapeDtypeStruct((pairs * PAIRS, 2 * PAIRS), F32),
        compiler_params=pltpu.CompilerParams(vmem_limit_bytes=VMEM_LIMIT),
        cost_estimate=pl.CostEstimate(
            flops=half2 * rows2 * NG, bytes_accessed=4 * response.size, transcendentals=0
        ),
    )(who, waves, response, first, second)


def sum_kernel(
    holders, members, part_ref, out_ref, got_ref, all_ref, send1, recv1, send2, recv2, send3, recv3
):
    ka = lax.axis_index("ka")
    ga = lax.axis_index("ga")
    size = part_ref.shape[0] // members
    mesh_id = pl.DeviceIdType.MESH
    barrier = pltpu.get_barrier_semaphore()

    def member(d):
        return lax.rem(ga + d, members)

    def holder(e):
        return lax.rem(ka + e, holders)

    def block(place):
        return pl.ds(pl.multiple_of(place * size, size), size)

    def scatter(d):
        return pltpu.make_async_remote_copy(
            src_ref=part_ref.at[block(member(d))],
            dst_ref=got_ref.at[d],
            send_sem=send1.at[d],
            recv_sem=recv1.at[d],
            device_id=(ka, member(d)),
            device_id_type=mesh_id,
        )

    def gather(d):
        return pltpu.make_async_remote_copy(
            src_ref=all_ref.at[ka, block(ga)],
            dst_ref=all_ref.at[ka, block(ga)],
            send_sem=send2.at[d],
            recv_sem=recv2.at[d],
            device_id=(ka, member(d)),
            device_id_type=mesh_id,
        )

    def exchange(e):
        return pltpu.make_async_remote_copy(
            src_ref=all_ref.at[ka],
            dst_ref=all_ref.at[ka],
            send_sem=send3.at[e],
            recv_sem=recv3.at[e],
            device_id=(holder(e), ga),
            device_id_type=mesh_id,
        )

    def loop(count, body):
        def run(i, carry):
            body(i)
            return carry

        lax.fori_loop(1, count, run, 0)

    def greet(device):
        pl.semaphore_signal(barrier, inc=1, device_id=device, device_id_type=mesh_id)

    loop(members, lambda d: greet((ka, member(d))))
    loop(holders, lambda e: greet((holder(e), ga)))
    pl.semaphore_wait(barrier, members + holders - 2)

    loop(members, lambda d: scatter(d).start())
    all_ref[ka, block(ga), :] = part_ref[block(ga), :]

    def add(d):
        scatter(d).wait_recv()
        all_ref[ka, block(ga), :] += got_ref[d]

    loop(members, add)
    loop(members, lambda d: gather(d).start())
    loop(members, lambda d: gather(d).wait_recv())
    loop(holders, lambda e: exchange(e).start())
    loop(members, lambda d: scatter(d).wait_send())
    loop(members, lambda d: gather(d).wait_send())
    loop(holders, lambda e: exchange(e).wait())
    out_ref[...] = all_ref[...]


def summed_everywhere(part, holders, members):
    rows, lanes = part.shape
    size = rows // members
    return pl.pallas_call(
        functools.partial(sum_kernel, holders, members),
        out_shape=jax.ShapeDtypeStruct((holders, rows, lanes), F32),
        in_specs=[pl.BlockSpec(memory_space=pltpu.VMEM)],
        out_specs=pl.BlockSpec(memory_space=pltpu.VMEM),
        scratch_shapes=[
            pltpu.VMEM((members, size, lanes), F32),
            pltpu.VMEM((holders, rows, lanes), F32),
        ]
        + [pltpu.SemaphoreType.DMA((members,))] * 4
        + [pltpu.SemaphoreType.DMA((holders,))] * 2,
        compiler_params=pltpu.CompilerParams(
            collective_id=0, has_side_effects=True, vmem_limit_bytes=VMEM_LIMIT
        ),
    )(part)


def mirror_kernel(source_ref, blocks_ref, out_ref):
    del source_ref

    def swapped(size, axis):
        row = lax.broadcasted_iota(jnp.int32, (size, size), axis)
        column = lax.broadcasted_iota(jnp.int32, (size, size), 1 - axis)
        inner = row % PAIRS
        return (column == row - inner + (inner % 8) * 8 + inner // 8).astype(F32)

    highest = lax.Precision.HIGHEST
    left = jnp.dot(swapped(PAIRS, 0), blocks_ref[0], precision=highest)
    both = jnp.dot(left, swapped(2 * PAIRS, 1), precision=highest)
    lane = lax.broadcasted_iota(jnp.int32, both.shape, 1)
    out_ref[0] = jnp.where(lane < PAIRS, both, -both)


def mirrored(source, blocks):
    shape = (1,) + blocks.shape[1:]
    spec = pltpu.PrefetchScalarGridSpec(
        num_scalar_prefetch=1,
        grid=(source.shape[0],),
        in_specs=[pl.BlockSpec(shape, lambda i, source: (source[i], 0, 0))],
        out_specs=pl.BlockSpec(shape, lambda i, source: (i, 0, 0)),
    )
    return pl.pallas_call(
        mirror_kernel,
        grid_spec=spec,
        out_shape=jax.ShapeDtypeStruct((source.shape[0],) + blocks.shape[1:], F32),
    )(source, blocks)


def local_tables(gmap, place, rows):
    columns = rows // NZ
    number = place * columns + jnp.arange(columns, dtype=jnp.int32)
    gx, gy = number // NY, number % NY
    r = jnp.arange(NXY, dtype=jnp.int32)
    turns = ((r // NY)[:, None] * gx[None] + (r % NY)[:, None] * gy[None]) % NX
    angle = turns.astype(F32) * (-2.0 * math.pi / NX)
    plane = SCALE_16 * jnp.stack([jnp.cos(angle), jnp.sin(angle)], axis=1)
    same = jnp.asarray(np.eye(STEP_Z), F32)
    first = same[:, None, :, None, None] * plane[None, :, None]
    first = first.reshape(STEP_Z * NXY, STEP_Z * 2 * columns).astype(BF)
    gz = lax.dynamic_slice_in_dim(gmap, place * rows, rows) % NZ
    z = jnp.arange(NZ, dtype=jnp.int32)
    angle = (z[:, None] * gz[None] % NZ).astype(F32) * (-2.0 * math.pi / NZ)
    c, s = SCALE_32 * jnp.cos(angle), SCALE_32 * jnp.sin(angle)
    line = jnp.stack([jnp.stack([c, s], axis=1), jnp.stack([-s, c], axis=1)], axis=1)
    own = (jnp.arange(rows) // NZ)[None, :] == jnp.arange(columns)[:, None]
    second = jnp.where(own[None, None, :, None, :], line[:, :, None], 0.0)
    second = second.reshape(NZ // STEP_Z, STEP_Z * 2 * columns, 2 * rows).astype(BF)
    return first, second


def flattened(blocks):
    number = blocks.shape[0]
    parts = blocks.reshape(number, PAIRS, 2, PAIRS).transpose(0, 2, 1, 3)
    return parts.reshape(number, 2, PAIRS * PAIRS)


def on_device(holders, members, wavefunctions, partner, gmap, screened):
    pairs, _, _, planes, _ = wavefunctions.shape
    ka_place = lax.axis_index("ka")
    ga_place = lax.axis_index("ga")
    owned = ka_place * pairs + jnp.arange(pairs, dtype=jnp.int32)
    wanted = partner[owned]
    by_plane = wavefunctions.transpose(3, 0, 1, 2, 4)
    val = by_plane[:, :, :, :NV].reshape(planes, pairs, 2 * NV, NXY)
    cond = by_plane[:, :, :, NV:].reshape(planes, pairs, 2 * NC, NXY)
    val = lax.all_gather(val, "ga", axis=0, tiled=True)
    inter = transformed_interaction(gmap, screened)
    first, second = local_tables(gmap, ga_place, screened.shape[0])
    val, cond, inter, first, second = lax.optimization_barrier((val, cond, inter, first, second))
    val = lax.all_gather(val, "ka", axis=0)
    cond = lax.all_gather(cond, "ga", axis=0, tiled=True)
    who = jnp.concatenate([ka_place[None].astype(jnp.int32), wanted // pairs, wanted % pairs])
    response = all_responses(who, val, inter)
    cond, response = lax.optimization_barrier((cond, response))
    cond = lax.all_gather(cond, "ka", axis=0)
    part = partial_blocks(who, cond, response, first, second)
    everyone = summed_everywhere(part, holders, members)
    everyone = everyone.reshape(holders * pairs, PAIRS, 2 * PAIRS)
    source = jnp.sum(
        jnp.where(
            partner[None, :] == owned[:, None],
            jnp.arange(partner.shape[0], dtype=jnp.int32)[None],
            0,
        ),
        axis=1,
    )
    own = lax.dynamic_slice_in_dim(everyone, ka_place * pairs, pairs)
    return (flattened(own), flattened(mirrored(source, everyone)))


def solution(mesh):
    in_specs = (P("ka", None, None, "ga", None), P(), P(), P("ga", None))
    out_specs = (P("ka", None, None), P("ka", None, None))
    return jax.shard_map(
        functools.partial(on_device, mesh.shape["ka"], mesh.shape["ga"]),
        mesh=mesh,
        in_specs=in_specs,
        out_specs=out_specs,
        check_vma=False,
    )
```

```python
import functools
import math

import jax
import jax.numpy as jnp
import numpy as np
from jax import lax
from jax.experimental import pallas as pl
from jax.experimental.pallas import tpu as pltpu
from jax.sharding import PartitionSpec as P

NV = 8
NC = 8
NX = 16
NY = 16
NZ = 32
NXY = NX * NY
NG = NXY * NZ
PAIRS = 64
GROUP = 256
SECOND_STAGE = 17
THIRD_STAGE = 25
STEP_Z = 8
BF = jnp.bfloat16
F32 = jnp.float32
VMEM_LIMIT = 56 * 1024 * 1024
SCALE_16 = 1.1329
SCALE_32 = 1.6245


def split(values):
    high = values.astype(BF)
    return high, (values - high.astype(F32)).astype(BF)


def line_table():
    z = np.arange(NZ)
    angle = -2.0 * np.pi * (z[:, None] * z[None, :] % NZ) / NZ
    return SCALE_32 * np.concatenate([np.cos(angle), np.sin(angle)], axis=0)


def plane_table():
    r = np.arange(NXY)
    x, y = r // NY, r % NY
    turns = (x[:, None] * x[None, :] % NX) / NX + (y[:, None] * y[None, :] % NY) / NY
    c, s = np.cos(-2.0 * np.pi * turns), np.sin(-2.0 * np.pi * turns)
    return SCALE_16 * np.block([[c, -s], [s, c]])


def gather_stages(holders, members, shards, wholes, sems):
    far, near, across, own = sems
    ka = lax.axis_index("ka")
    ga = lax.axis_index("ga")
    firsts = members // 4
    first, quad = ga // 4, ga % 4
    by_one = quad + 1 - 2 * (quad % 2)
    by_two = (quad + 2) % 4
    by_both = (by_one + 2) % 4
    mesh_id = pl.DeviceIdType.MESH
    barrier = pltpu.get_barrier_semaphore()
    orders = ((by_one, by_two), (by_two, by_one))

    def remote(src, dst, send, recv, device):
        return pltpu.make_async_remote_copy(
            src_ref=src,
            dst_ref=dst,
            send_sem=send,
            recv_sem=recv,
            device_id=device,
            device_id_type=mesh_id,
        )

    def over_first(h, d):
        target = ((first + d) % firsts) * 4 + quad
        dst = wholes[h].at[ka, first, quad]
        return remote(shards[h], dst, far.at[0, h, d], far.at[1, h, d], (ka, target))

    def in_quad(h, index):
        place = (quad, quad, orders[h][0])[index]
        target = first * 4 + orders[h][0 if index == 0 else 1]
        block = wholes[h].at[ka, :, place]
        return remote(block, block, near.at[0, h, index], near.at[1, h, index], (ka, target))

    def to_holder(h, index, e):
        place = (quad, orders[h][0], orders[h][1], by_both)[index]
        block = wholes[h].at[ka, :, place]
        device = ((ka + e) % holders, ga)
        return remote(block, block, across.at[0, h, index, e], across.at[1, h, index, e], device)

    def place_own(h):
        return pltpu.make_async_copy(shards[h], wholes[h].at[ka, first, quad], own.at[h])

    def greet(device):
        pl.semaphore_signal(barrier, inc=1, device_id=device, device_id_type=mesh_id)

    distances = range(1, firsts)
    others = range(1, holders)

    def enter():
        for d in distances:
            greet((ka, ((first + d) % firsts) * 4 + quad))
        for place in (by_one, by_two):
            greet((ka, first * 4 + place))
        for e in others:
            greet(((ka + e) % holders, ga))
        pl.semaphore_wait(barrier, firsts - 1 + 2 + holders - 1)
        for h in range(2):
            for d in distances:
                over_first(h, d).start()
            place_own(h).start()

    def second():
        for h in range(2):
            place_own(h).wait()
            for d in distances:
                over_first(h, d).wait_recv()
            in_quad(h, 0).start()
            for e in others:
                to_holder(h, 0, e).start()

    def third():
        for h in range(2):
            in_quad(h, 0).wait_recv()
            in_quad(h, 1).start()
            in_quad(h, 2).start()
            for e in others:
                to_holder(h, 1, e).start()

    def leave():
        for h in range(2):
            for index in (1, 2):
                in_quad(h, index).wait_recv()
                for e in others:
                    to_holder(h, index + 1, e).start()
        for h in range(2):
            for d in distances:
                over_first(h, d).wait_send()
            for index in range(3):
                in_quad(h, index).wait_send()
            for index in range(4):
                for e in others:
                    to_holder(h, index, e).wait()

    return enter, second, third, leave


def interaction_kernel(
    steps,
    holders,
    members,
    line_ref,
    plane_ref,
    gz_ref,
    w_ref,
    val_ref,
    cond_ref,
    out_ref,
    all_val_ref,
    all_cond_ref,
    mid_ref,
    low_ref,
    *sems,
):
    step = pl.program_id(0)
    rows = w_ref.shape[0]
    per = w_ref.shape[1] // GROUP
    cols = GROUP // NZ
    enter, second, third, leave = gather_stages(
        holders, members, (val_ref, cond_ref), (all_val_ref, all_cond_ref), sems
    )
    pl.when(step == 0)(enter)
    pl.when(step == SECOND_STAGE)(second)
    pl.when(step == THIRD_STAGE)(third)

    @pl.when(step < steps)
    def _():
        parts = []
        for g in range(per):
            gz = gz_ref[0, :, g * GROUP : (g + 1) * GROUP]
            hot = lax.broadcasted_iota(jnp.int32, (NZ, GROUP), 0) == gz
            table = jnp.dot(line_ref[...], hot.astype(F32).astype(BF), preferred_element_type=F32)
            column = lax.broadcasted_iota(jnp.int32, (cols, GROUP), 1) // NZ
            mask = column == lax.broadcasted_iota(jnp.int32, (cols, GROUP), 0)
            wide = jnp.where(mask[None], table[:, None, :], 0.0)
            wide = wide.reshape(2 * NZ * cols, GROUP).astype(BF)
            got = lax.dot_general(
                wide,
                w_ref[:, g * GROUP : (g + 1) * GROUP],
                (((1,), (1,)), ((), ())),
                preferred_element_type=F32,
            )
            parts.append(got.reshape(2, NZ, cols, rows))
        high, low = split(jnp.concatenate(parts, axis=2))
        start = pl.multiple_of(step * (per * cols), per * cols)
        for p in range(2):
            mid_ref[:, p, pl.ds(start, per * cols), :] = high[p]
            low_ref[:, p, pl.ds(start, per * cols), :] = low[p]

    @pl.when(step >= steps)
    def _():
        planes = out_ref.shape[0]
        for i in range(planes):
            z = (step - steps) * planes + i
            mid = mid_ref[z].reshape(2 * NXY, rows)
            low = low_ref[z].reshape(2 * NXY, rows)
            got = jnp.dot(plane_ref[...], mid, preferred_element_type=F32)
            got = (got + jnp.dot(plane_ref[...], low, preferred_element_type=F32)).astype(BF)
            out_ref[i, :, :rows] = got[:NXY]
            out_ref[i, :, rows:] = got[NXY:]

    pl.when(step == pl.num_programs(0) - 1)(leave)


def transformed_interaction(holders, members, gmap, screened, val, cond):
    rows = screened.shape[0]
    per = 2
    steps = NG // (GROUP * per)
    planes = 2
    gz = (gmap % NZ).reshape(steps, 1, GROUP * per)
    last = steps - 1
    whole = jax.ShapeDtypeStruct((holders, members // 4, 4) + val.shape, BF)
    dma = pltpu.SemaphoreType.DMA
    anywhere = pl.BlockSpec(memory_space=pl.ANY)
    inter, val, cond = pl.pallas_call(
        functools.partial(interaction_kernel, steps, holders, members),
        grid=(steps + NZ // planes,),
        in_specs=[
            pl.BlockSpec((2 * NZ, NZ), lambda i: (0, 0)),
            pl.BlockSpec((2 * NXY, 2 * NXY), lambda i: (0, 0)),
            pl.BlockSpec((1, 1, GROUP * per), lambda i: (jnp.minimum(i, last), 0, 0)),
            pl.BlockSpec((rows, GROUP * per), lambda i: (0, jnp.minimum(i, last))),
            anywhere,
            anywhere,
        ],
        out_specs=[
            pl.BlockSpec((planes, NXY, 2 * rows), lambda i: (jnp.maximum(i - steps, 0), 0, 0)),
            anywhere,
            anywhere,
        ],
        out_shape=[jax.ShapeDtypeStruct((NZ, NXY, 2 * rows), BF), whole, whole],
        scratch_shapes=[
            pltpu.VMEM((NZ, 2, NXY, rows), BF),
            pltpu.VMEM((NZ, 2, NXY, rows), BF),
            dma((2, 2, members // 4)),
            dma((2, 2, 3)),
            dma((2, 2, 4, holders)),
            dma((2,)),
        ],
        compiler_params=pltpu.CompilerParams(
            collective_id=1, has_side_effects=True, vmem_limit_bytes=VMEM_LIMIT
        ),
        cost_estimate=pl.CostEstimate(
            flops=16 * NXY * NG * rows, bytes_accessed=6 * NG * rows, transcendentals=0
        ),
    )(
        jnp.asarray(line_table(), BF),
        jnp.asarray(plane_table(), BF),
        gz,
        screened,
        val,
        cond,
    )
    shape = (holders, NZ) + val.shape[4:]
    return inter, val.reshape(shape), cond.reshape(shape)


def pair_rows(left, right):
    left_real, left_imag = left
    right_real, right_imag = right
    real_part = [
        left_real[b : b + 1] * right_real + left_imag[b : b + 1] * right_imag for b in range(8)
    ]
    imag_part = [
        left_real[b : b + 1] * right_imag - left_imag[b : b + 1] * right_real for b in range(8)
    ]
    return (
        jnp.concatenate(real_part, axis=0),
        jnp.concatenate(imag_part, axis=0),
    )


def fill_planes(who_ref, waves_ref, pairs, store):
    def fill(k, carry):
        for z in range(STEP_Z):
            home = waves_ref[who_ref[0], z, k].astype(F32)
            away = waves_ref[who_ref[1 + k], z, who_ref[1 + pairs + k]].astype(F32)
            real_part, imag_part = pair_rows((home[:8], home[8:]), (away[:8], away[8:]))
            lanes = slice(z * NXY, (z + 1) * NXY)
            start = pl.multiple_of(k * PAIRS, PAIRS)
            store(pl.ds(start, PAIRS), lanes, real_part)
            store(pl.ds(pairs * PAIRS + start, PAIRS), lanes, imag_part)
        return carry

    lax.fori_loop(0, pairs, fill, 0)


def response_kernel(pairs, who_ref, waves_ref, inter_ref, out_ref, val_ref):
    def store(rows, lanes, values):
        val_ref[rows, lanes] = values.astype(BF)

    fill_planes(who_ref, waves_ref, pairs, store)

    @pl.when(pl.program_id(0) == 0)
    def _():
        out_ref[...] = jnp.zeros_like(out_ref)

    inter = inter_ref[...].reshape(STEP_Z * NXY, inter_ref.shape[2])
    out_ref[...] += jnp.dot(val_ref[...], inter, preferred_element_type=F32)


def block_kernel(
    pairs,
    who_ref,
    waves_ref,
    response_ref,
    first_ref,
    second_ref,
    out_ref,
    cond_ref,
    cond_low_ref,
    spectrum_ref,
):
    step = pl.program_id(0)
    half = pairs * PAIRS
    rows = response_ref.shape[1] // 2

    def store(where, lanes, values):
        high, low = split(values)
        cond_ref[where, lanes] = high
        cond_low_ref[where, lanes] = low

    fill_planes(who_ref, waves_ref, pairs, store)

    @pl.when(step == 0)
    def _():
        spectrum_ref[...] = jnp.zeros_like(spectrum_ref)

    mixed = jnp.dot(cond_ref[...], first_ref[...], preferred_element_type=F32)
    mixed = mixed + jnp.dot(cond_low_ref[...], first_ref[...], preferred_element_type=F32)
    mixed, mixed_low = split(mixed)
    spectrum_ref[...] += jnp.dot(mixed, second_ref[0], preferred_element_type=F32) + jnp.dot(
        mixed_low, second_ref[0], preferred_element_type=F32
    )

    @pl.when(step == pl.num_programs(0) - 1)
    def _():
        def finish(k, carry):
            start = pl.multiple_of(k * PAIRS, PAIRS)
            top = pl.ds(start, PAIRS)
            low = pl.ds(half + start, PAIRS)

            def whole(ref):
                real_part = ref[top, :rows] - ref[low, rows:]
                imag_part = ref[top, rows:] + ref[low, :rows]
                return split(jnp.concatenate([real_part, imag_part], axis=0))

            def mixed_product(left, right):
                return lax.dot_general(
                    left, right, (((1,), (1,)), ((), ())), preferred_element_type=F32
                )

            cond, cond_low = whole(spectrum_ref)
            resp, resp_low = whole(response_ref)
            product = mixed_product(cond, resp)
            product = product + mixed_product(cond_low, resp) + mixed_product(cond, resp_low)
            scale = 1.0 / (NG * (SCALE_16 * SCALE_32) ** 2)
            a, b = product[:PAIRS], product[PAIRS:]
            real_part = a[:, :PAIRS] + b[:, PAIRS:]
            imag_part = a[:, PAIRS:] - b[:, :PAIRS]
            out_ref[top, :] = jnp.concatenate([real_part, imag_part], axis=1) * scale
            return carry

        lax.fori_loop(0, pairs, finish, 0)


def waves_spec(waves):
    shape = (waves.shape[0], STEP_Z) + waves.shape[2:]
    return pl.BlockSpec(shape, lambda i, who: (0, i, 0, 0, 0))


def all_responses(who, waves, inter):
    pairs = waves.shape[2]
    rows2 = inter.shape[2]
    half2 = 2 * pairs * PAIRS
    spec = pltpu.PrefetchScalarGridSpec(
        num_scalar_prefetch=1,
        grid=(NZ // STEP_Z,),
        in_specs=[
            waves_spec(waves),
            pl.BlockSpec((STEP_Z, NXY, rows2), lambda i, who: (i, 0, 0)),
        ],
        out_specs=pl.BlockSpec((half2, rows2), lambda i, who: (0, 0)),
        scratch_shapes=[pltpu.VMEM((half2, STEP_Z * NXY), BF)],
    )
    return pl.pallas_call(
        functools.partial(response_kernel, pairs),
        grid_spec=spec,
        out_shape=jax.ShapeDtypeStruct((half2, rows2), F32),
        compiler_params=pltpu.CompilerParams(vmem_limit_bytes=VMEM_LIMIT),
        cost_estimate=pl.CostEstimate(
            flops=2 * half2 * rows2 * NG, bytes_accessed=2 * inter.size, transcendentals=0
        ),
    )(who, waves, inter)


def partial_blocks(who, waves, response, first, second):
    pairs = waves.shape[2]
    half2, rows2 = response.shape
    spec = pltpu.PrefetchScalarGridSpec(
        num_scalar_prefetch=1,
        grid=(NZ // STEP_Z,),
        in_specs=[
            waves_spec(waves),
            pl.BlockSpec((half2, rows2), lambda i, who: (0, 0)),
            pl.BlockSpec(first.shape, lambda i, who: (0, 0)),
            pl.BlockSpec((1,) + second.shape[1:], lambda i, who: (i, 0, 0)),
        ],
        out_specs=pl.BlockSpec((pairs * PAIRS, 2 * PAIRS), lambda i, who: (0, 0)),
        scratch_shapes=[
            pltpu.VMEM((half2, STEP_Z * NXY), BF),
            pltpu.VMEM((half2, STEP_Z * NXY), BF),
            pltpu.VMEM((half2, rows2), F32),
        ],
    )
    return pl.pallas_call(
        functools.partial(block_kernel, pairs),
        grid_spec=spec,
        out_shape=jax.ShapeDtypeStruct((pairs * PAIRS, 2 * PAIRS), F32),
        compiler_params=pltpu.CompilerParams(vmem_limit_bytes=VMEM_LIMIT),
        cost_estimate=pl.CostEstimate(
            flops=half2 * rows2 * NG, bytes_accessed=4 * response.size, transcendentals=0
        ),
    )(who, waves, response, first, second)


def sum_kernel(
    holders, members, part_ref, out_ref, got_ref, all_ref, send1, recv1, send2, recv2, send3, recv3
):
    ka = lax.axis_index("ka")
    ga = lax.axis_index("ga")
    size = part_ref.shape[0] // members
    mesh_id = pl.DeviceIdType.MESH
    barrier = pltpu.get_barrier_semaphore()

    def member(d):
        return lax.rem(ga + d, members)

    def holder(e):
        return lax.rem(ka + e, holders)

    def block(place):
        return pl.ds(pl.multiple_of(place * size, size), size)

    def scatter(d):
        return pltpu.make_async_remote_copy(
            src_ref=part_ref.at[block(member(d))],
            dst_ref=got_ref.at[d],
            send_sem=send1.at[d],
            recv_sem=recv1.at[d],
            device_id=(ka, member(d)),
            device_id_type=mesh_id,
        )

    def gather(d):
        return pltpu.make_async_remote_copy(
            src_ref=all_ref.at[ka, block(ga)],
            dst_ref=all_ref.at[ka, block(ga)],
            send_sem=send2.at[d],
            recv_sem=recv2.at[d],
            device_id=(ka, member(d)),
            device_id_type=mesh_id,
        )

    def exchange(e):
        return pltpu.make_async_remote_copy(
            src_ref=all_ref.at[ka],
            dst_ref=all_ref.at[ka],
            send_sem=send3.at[e],
            recv_sem=recv3.at[e],
            device_id=(holder(e), ga),
            device_id_type=mesh_id,
        )

    def loop(count, body):
        def run(i, carry):
            body(i)
            return carry

        lax.fori_loop(1, count, run, 0)

    def greet(device):
        pl.semaphore_signal(barrier, inc=1, device_id=device, device_id_type=mesh_id)

    loop(members, lambda d: greet((ka, member(d))))
    loop(holders, lambda e: greet((holder(e), ga)))
    pl.semaphore_wait(barrier, members + holders - 2)

    loop(members, lambda d: scatter(d).start())
    all_ref[ka, block(ga), :] = part_ref[block(ga), :]

    def add(d):
        scatter(d).wait_recv()
        all_ref[ka, block(ga), :] += got_ref[d]

    loop(members, add)
    loop(members, lambda d: gather(d).start())
    loop(members, lambda d: gather(d).wait_recv())
    loop(holders, lambda e: exchange(e).start())
    loop(members, lambda d: scatter(d).wait_send())
    loop(members, lambda d: gather(d).wait_send())
    loop(holders, lambda e: exchange(e).wait())
    out_ref[...] = all_ref[...]


def summed_everywhere(part, holders, members):
    rows, lanes = part.shape
    size = rows // members
    return pl.pallas_call(
        functools.partial(sum_kernel, holders, members),
        out_shape=jax.ShapeDtypeStruct((holders, rows, lanes), F32),
        in_specs=[pl.BlockSpec(memory_space=pltpu.VMEM)],
        out_specs=pl.BlockSpec(memory_space=pltpu.VMEM),
        scratch_shapes=[
            pltpu.VMEM((members, size, lanes), F32),
            pltpu.VMEM((holders, rows, lanes), F32),
        ]
        + [pltpu.SemaphoreType.DMA((members,))] * 4
        + [pltpu.SemaphoreType.DMA((holders,))] * 2,
        compiler_params=pltpu.CompilerParams(
            collective_id=0, has_side_effects=True, vmem_limit_bytes=VMEM_LIMIT
        ),
    )(part)


def mirror_kernel(source_ref, blocks_ref, out_ref):
    del source_ref

    def swapped(size, axis):
        row = lax.broadcasted_iota(jnp.int32, (size, size), axis)
        column = lax.broadcasted_iota(jnp.int32, (size, size), 1 - axis)
        inner = row % PAIRS
        return (column == row - inner + (inner % 8) * 8 + inner // 8).astype(F32)

    highest = lax.Precision.HIGHEST
    left = jnp.dot(swapped(PAIRS, 0), blocks_ref[0], precision=highest)
    both = jnp.dot(left, swapped(2 * PAIRS, 1), precision=highest)
    lane = lax.broadcasted_iota(jnp.int32, both.shape, 1)
    out_ref[0] = jnp.where(lane < PAIRS, both, -both)


def mirrored(source, blocks):
    shape = (1,) + blocks.shape[1:]
    spec = pltpu.PrefetchScalarGridSpec(
        num_scalar_prefetch=1,
        grid=(source.shape[0],),
        in_specs=[pl.BlockSpec(shape, lambda i, source: (source[i], 0, 0))],
        out_specs=pl.BlockSpec(shape, lambda i, source: (i, 0, 0)),
    )
    return pl.pallas_call(
        mirror_kernel,
        grid_spec=spec,
        out_shape=jax.ShapeDtypeStruct((source.shape[0],) + blocks.shape[1:], F32),
    )(source, blocks)


def local_tables(gmap, place, rows):
    columns = rows // NZ
    number = place * columns + jnp.arange(columns, dtype=jnp.int32)
    gx, gy = number // NY, number % NY
    r = jnp.arange(NXY, dtype=jnp.int32)
    turns = ((r // NY)[:, None] * gx[None] + (r % NY)[:, None] * gy[None]) % NX
    angle = turns.astype(F32) * (-2.0 * math.pi / NX)
    plane = SCALE_16 * jnp.stack([jnp.cos(angle), jnp.sin(angle)], axis=1)
    same = jnp.asarray(np.eye(STEP_Z), F32)
    first = same[:, None, :, None, None] * plane[None, :, None]
    first = first.reshape(STEP_Z * NXY, STEP_Z * 2 * columns).astype(BF)
    gz = lax.dynamic_slice_in_dim(gmap, place * rows, rows) % NZ
    z = jnp.arange(NZ, dtype=jnp.int32)
    angle = (z[:, None] * gz[None] % NZ).astype(F32) * (-2.0 * math.pi / NZ)
    c, s = SCALE_32 * jnp.cos(angle), SCALE_32 * jnp.sin(angle)
    line = jnp.stack([jnp.stack([c, s], axis=1), jnp.stack([-s, c], axis=1)], axis=1)
    own = (jnp.arange(rows) // NZ)[None, :] == jnp.arange(columns)[:, None]
    second = jnp.where(own[None, None, :, None, :], line[:, :, None], 0.0)
    second = second.reshape(NZ // STEP_Z, STEP_Z * 2 * columns, 2 * rows).astype(BF)
    return first, second


def flattened(blocks):
    number = blocks.shape[0]
    parts = blocks.reshape(number, PAIRS, 2, PAIRS).transpose(0, 2, 1, 3)
    return parts.reshape(number, 2, PAIRS * PAIRS)


def on_device(holders, members, wavefunctions, partner, gmap, screened):
    pairs, _, _, planes, _ = wavefunctions.shape
    ka_place = lax.axis_index("ka")
    ga_place = lax.axis_index("ga")
    owned = ka_place * pairs + jnp.arange(pairs, dtype=jnp.int32)
    wanted = partner[owned]
    by_plane = wavefunctions.transpose(3, 0, 1, 2, 4)
    val = by_plane[:, :, :, :NV].reshape(planes, pairs, 2 * NV, NXY)
    cond = by_plane[:, :, :, NV:].reshape(planes, pairs, 2 * NC, NXY)
    inter, val, cond = transformed_interaction(holders, members, gmap, screened, val, cond)
    first, second = local_tables(gmap, ga_place, screened.shape[0])
    who = jnp.concatenate([ka_place[None].astype(jnp.int32), wanted // pairs, wanted % pairs])
    response = all_responses(who, val, inter)
    part = partial_blocks(who, cond, response, first, second)
    everyone = summed_everywhere(part, holders, members)
    everyone = everyone.reshape(holders * pairs, PAIRS, 2 * PAIRS)
    source = jnp.sum(
        jnp.where(
            partner[None, :] == owned[:, None],
            jnp.arange(partner.shape[0], dtype=jnp.int32)[None],
            0,
        ),
        axis=1,
    )
    own = lax.dynamic_slice_in_dim(everyone, ka_place * pairs, pairs)
    return (flattened(own), flattened(mirrored(source, everyone)))


def solution(mesh):
    in_specs = (P("ka", None, None, "ga", None), P(), P(), P("ga", None))
    out_specs = (P("ka", None, None), P("ka", None, None))
    return jax.shard_map(
        functools.partial(on_device, mesh.shape["ka"], mesh.shape["ga"]),
        mesh=mesh,
        in_specs=in_specs,
        out_specs=out_specs,
        check_vma=False,
    )
```

```python
import functools
import math

import jax
import jax.numpy as jnp
import numpy as np
from jax import lax
from jax.experimental import pallas as pl
from jax.experimental.pallas import tpu as pltpu
from jax.sharding import PartitionSpec as P

NV = 8
NC = 8
NX = 16
NY = 16
NZ = 32
NXY = NX * NY
NG = NXY * NZ
PAIRS = 64
GROUP = 256
SECOND_STAGE = 17
THIRD_STAGE = 25
STEP_Z = 8
BF = jnp.bfloat16
F32 = jnp.float32
VMEM_LIMIT = 56 * 1024 * 1024
SCALE_16 = 1.1329
SCALE_32 = 1.6245


def split(values):
    high = values.astype(BF)
    return high, (values - high.astype(F32)).astype(BF)


def line_table():
    z = np.arange(NZ)
    angle = -2.0 * np.pi * (z[:, None] * z[None, :] % NZ) / NZ
    return SCALE_32 * np.concatenate([np.cos(angle), np.sin(angle)], axis=0)


def plane_table():
    r = np.arange(NXY)
    x, y = r // NY, r % NY
    turns = (x[:, None] * x[None, :] % NX) / NX + (y[:, None] * y[None, :] % NY) / NY
    c, s = np.cos(-2.0 * np.pi * turns), np.sin(-2.0 * np.pi * turns)
    return SCALE_16 * np.block([[c, -s], [s, c]])


def gather_stages(holders, members, shards, wholes, sems):
    far, near, across, own = sems
    ka = lax.axis_index("ka")
    ga = lax.axis_index("ga")
    firsts = members // 4
    first, quad = ga // 4, ga % 4
    by_one = quad + 1 - 2 * (quad % 2)
    by_two = (quad + 2) % 4
    by_both = (by_one + 2) % 4
    mesh_id = pl.DeviceIdType.MESH
    barrier = pltpu.get_barrier_semaphore()
    orders = ((by_one, by_two), (by_two, by_one))

    def remote(src, dst, send, recv, device):
        return pltpu.make_async_remote_copy(
            src_ref=src,
            dst_ref=dst,
            send_sem=send,
            recv_sem=recv,
            device_id=device,
            device_id_type=mesh_id,
        )

    def over_first(h, d):
        target = ((first + d) % firsts) * 4 + quad
        dst = wholes[h].at[ka, first, quad]
        return remote(shards[h], dst, far.at[0, h, d], far.at[1, h, d], (ka, target))

    def in_quad(h, index):
        place = (quad, quad, orders[h][0])[index]
        target = first * 4 + orders[h][0 if index == 0 else 1]
        block = wholes[h].at[ka, :, place]
        return remote(block, block, near.at[0, h, index], near.at[1, h, index], (ka, target))

    def to_holder(h, index, e):
        place = (quad, orders[h][0], orders[h][1], by_both)[index]
        block = wholes[h].at[ka, :, place]
        device = ((ka + e) % holders, ga)
        return remote(block, block, across.at[0, h, index, e], across.at[1, h, index, e], device)

    def place_own(h):
        return pltpu.make_async_copy(shards[h], wholes[h].at[ka, first, quad], own.at[h])

    def greet(device):
        pl.semaphore_signal(barrier, inc=1, device_id=device, device_id_type=mesh_id)

    distances = range(1, firsts)
    others = range(1, holders)

    def enter():
        for d in distances:
            greet((ka, ((first + d) % firsts) * 4 + quad))
        for place in (by_one, by_two):
            greet((ka, first * 4 + place))
        for e in others:
            greet(((ka + e) % holders, ga))
        pl.semaphore_wait(barrier, firsts - 1 + 2 + holders - 1)
        for h in range(2):
            for d in distances:
                over_first(h, d).start()
            place_own(h).start()

    def second():
        for h in range(2):
            place_own(h).wait()
            for d in distances:
                over_first(h, d).wait_recv()
            in_quad(h, 0).start()
            for e in others:
                to_holder(h, 0, e).start()

    def third():
        for h in range(2):
            in_quad(h, 0).wait_recv()
            in_quad(h, 1).start()
            in_quad(h, 2).start()
            for e in others:
                to_holder(h, 1, e).start()

    def leave():
        for h in range(2):
            for index in (1, 2):
                in_quad(h, index).wait_recv()
                for e in others:
                    to_holder(h, index + 1, e).start()
        for h in range(2):
            for d in distances:
                over_first(h, d).wait_send()
            for index in range(3):
                in_quad(h, index).wait_send()
            for index in range(4):
                for e in others:
                    to_holder(h, index, e).wait()

    return enter, second, third, leave


def interaction_kernel(
    steps,
    holders,
    members,
    line_ref,
    plane_ref,
    gz_ref,
    w_ref,
    val_ref,
    cond_ref,
    out_ref,
    all_val_ref,
    all_cond_ref,
    mid_ref,
    low_ref,
    *sems,
):
    step = pl.program_id(0)
    rows = w_ref.shape[0]
    per = w_ref.shape[1] // GROUP
    cols = GROUP // NZ
    enter, second, third, leave = gather_stages(
        holders, members, (val_ref, cond_ref), (all_val_ref, all_cond_ref), sems
    )
    pl.when(step == 0)(enter)
    pl.when(step == SECOND_STAGE)(second)
    pl.when(step == THIRD_STAGE)(third)

    @pl.when(step < steps)
    def _():
        parts = []
        for g in range(per):
            gz = gz_ref[0, :, g * GROUP : (g + 1) * GROUP]
            hot = lax.broadcasted_iota(jnp.int32, (NZ, GROUP), 0) == gz
            table = jnp.dot(line_ref[...], hot.astype(F32).astype(BF), preferred_element_type=F32)
            column = lax.broadcasted_iota(jnp.int32, (cols, GROUP), 1) // NZ
            mask = column == lax.broadcasted_iota(jnp.int32, (cols, GROUP), 0)
            wide = jnp.where(mask[None], table[:, None, :], 0.0)
            wide = wide.reshape(2 * NZ * cols, GROUP).astype(BF)
            got = lax.dot_general(
                wide,
                w_ref[:, g * GROUP : (g + 1) * GROUP],
                (((1,), (1,)), ((), ())),
                preferred_element_type=F32,
            )
            parts.append(got.reshape(2, NZ, cols, rows))
        high, low = split(jnp.concatenate(parts, axis=2))
        start = pl.multiple_of(step * (per * cols), per * cols)
        for p in range(2):
            mid_ref[:, p, pl.ds(start, per * cols), :] = high[p]
            low_ref[:, p, pl.ds(start, per * cols), :] = low[p]

    @pl.when(step >= steps)
    def _():
        planes = out_ref.shape[0]
        for i in range(planes):
            z = (step - steps) * planes + i
            mid = mid_ref[z].reshape(2 * NXY, rows)
            low = low_ref[z].reshape(2 * NXY, rows)
            got = jnp.dot(plane_ref[...], mid, preferred_element_type=F32)
            got = (got + jnp.dot(plane_ref[...], low, preferred_element_type=F32)).astype(BF)
            out_ref[i, :, :rows] = got[:NXY]
            out_ref[i, :, rows:] = got[NXY:]

    pl.when(step == pl.num_programs(0) - 1)(leave)


def transformed_interaction(holders, members, gmap, screened, val, cond):
    rows = screened.shape[0]
    per = 2
    steps = NG // (GROUP * per)
    planes = 2
    gz = (gmap % NZ).reshape(steps, 1, GROUP * per)
    last = steps - 1
    whole = jax.ShapeDtypeStruct((holders, members // 4, 4) + val.shape, BF)
    dma = pltpu.SemaphoreType.DMA
    anywhere = pl.BlockSpec(memory_space=pl.ANY)
    inter, val, cond = pl.pallas_call(
        functools.partial(interaction_kernel, steps, holders, members),
        grid=(steps + NZ // planes,),
        in_specs=[
            pl.BlockSpec((2 * NZ, NZ), lambda i: (0, 0)),
            pl.BlockSpec((2 * NXY, 2 * NXY), lambda i: (0, 0)),
            pl.BlockSpec((1, 1, GROUP * per), lambda i: (jnp.minimum(i, last), 0, 0)),
            pl.BlockSpec((rows, GROUP * per), lambda i: (0, jnp.minimum(i, last))),
            anywhere,
            anywhere,
        ],
        out_specs=[
            pl.BlockSpec((planes, NXY, 2 * rows), lambda i: (jnp.maximum(i - steps, 0), 0, 0)),
            anywhere,
            anywhere,
        ],
        out_shape=[jax.ShapeDtypeStruct((NZ, NXY, 2 * rows), BF), whole, whole],
        scratch_shapes=[
            pltpu.VMEM((NZ, 2, NXY, rows), BF),
            pltpu.VMEM((NZ, 2, NXY, rows), BF),
            dma((2, 2, members // 4)),
            dma((2, 2, 3)),
            dma((2, 2, 4, holders)),
            dma((2,)),
        ],
        compiler_params=pltpu.CompilerParams(
            collective_id=1, has_side_effects=True, vmem_limit_bytes=VMEM_LIMIT
        ),
        cost_estimate=pl.CostEstimate(
            flops=16 * NXY * NG * rows, bytes_accessed=6 * NG * rows, transcendentals=0
        ),
    )(
        jnp.asarray(line_table(), BF),
        jnp.asarray(plane_table(), BF),
        gz,
        screened,
        val,
        cond,
    )
    shape = (holders, NZ) + val.shape[4:]
    return inter, val.reshape(shape), cond.reshape(shape)


def pair_rows(left, right):
    left_real, left_imag = left
    right_real, right_imag = right
    real_part = [
        left_real[b : b + 1] * right_real + left_imag[b : b + 1] * right_imag for b in range(8)
    ]
    imag_part = [
        left_real[b : b + 1] * right_imag - left_imag[b : b + 1] * right_real for b in range(8)
    ]
    return (
        jnp.concatenate(real_part, axis=0),
        jnp.concatenate(imag_part, axis=0),
    )


def fill_pair(who_ref, waves_ref, pairs, store):
    def fill(k, carry):
        for z in range(STEP_Z):
            home = waves_ref[who_ref[0], z, k].astype(F32)
            away = waves_ref[who_ref[1 + k], z, who_ref[1 + pairs + k]].astype(F32)
            real_part, imag_part = pair_rows((home[:8], home[8:]), (away[:8], away[8:]))
            lanes = slice(z * NXY, (z + 1) * NXY)
            start = pl.multiple_of(k * PAIRS, PAIRS)
            store(pl.ds(start, PAIRS), lanes, real_part)
            store(pl.ds(pairs * PAIRS + start, PAIRS), lanes, imag_part)
        return carry

    return fill


def response_kernel(pairs, who_ref, waves_ref, inter_ref, out_ref, even_ref, odd_ref):
    step = pl.program_id(0)
    steps = pl.num_programs(0) - 1
    width = 256
    chunks = out_ref.shape[1] // width
    each = pairs // chunks

    def work(fill_ref, dot_ref):
        def store(rows, lanes, values):
            fill_ref[rows, lanes] = values.astype(BF)

        fill = fill_pair(who_ref, waves_ref, pairs, store)

        def run(c, carry):
            if dot_ref is not None:
                lanes = pl.ds(pl.multiple_of(c * width, width), width)
                inter = inter_ref[:, :, lanes].reshape(STEP_Z * NXY, width)
                out_ref[:, lanes] += jnp.dot(dot_ref[...], inter, preferred_element_type=F32)
            if fill_ref is not None:
                for i in range(each):
                    fill(c * each + i, 0)
            return carry

        lax.fori_loop(0, chunks, run, 0)

    @pl.when(step == 0)
    def _():
        out_ref[...] = jnp.zeros_like(out_ref)
        work(even_ref, None)

    @pl.when((step % 2 == 1) & (step < steps))
    def _():
        work(odd_ref, even_ref)

    @pl.when((step % 2 == 0) & (step > 0) & (step < steps))
    def _():
        work(even_ref, odd_ref)

    @pl.when(step == steps)
    def _():
        work(None, odd_ref)


def block_kernel(
    pairs,
    who_ref,
    waves_ref,
    response_ref,
    first_ref,
    second_ref,
    out_ref,
    cond_ref,
    cond_low_ref,
    spectrum_ref,
):
    step = pl.program_id(0)
    half = pairs * PAIRS
    rows = response_ref.shape[1] // 2

    def store(where, lanes, values):
        high, low = split(values)
        cond_ref[where, lanes] = high
        cond_low_ref[where, lanes] = low

    lax.fori_loop(0, pairs, fill_pair(who_ref, waves_ref, pairs, store), 0)

    @pl.when(step == 0)
    def _():
        spectrum_ref[...] = jnp.zeros_like(spectrum_ref)

    mixed = jnp.dot(cond_ref[...], first_ref[...], preferred_element_type=F32)
    mixed = mixed + jnp.dot(cond_low_ref[...], first_ref[...], preferred_element_type=F32)
    mixed, mixed_low = split(mixed)
    spectrum_ref[...] += jnp.dot(mixed, second_ref[0], preferred_element_type=F32) + jnp.dot(
        mixed_low, second_ref[0], preferred_element_type=F32
    )

    @pl.when(step == pl.num_programs(0) - 1)
    def _():
        def finish(k, carry):
            start = pl.multiple_of(k * PAIRS, PAIRS)
            top = pl.ds(start, PAIRS)
            low = pl.ds(half + start, PAIRS)

            def whole(ref):
                real_part = ref[top, :rows] - ref[low, rows:]
                imag_part = ref[top, rows:] + ref[low, :rows]
                return split(jnp.concatenate([real_part, imag_part], axis=0))

            def mixed_product(left, right):
                return lax.dot_general(
                    left, right, (((1,), (1,)), ((), ())), preferred_element_type=F32
                )

            cond, cond_low = whole(spectrum_ref)
            resp, resp_low = whole(response_ref)
            product = mixed_product(cond, resp)
            product = product + mixed_product(cond_low, resp) + mixed_product(cond, resp_low)
            scale = 1.0 / (NG * (SCALE_16 * SCALE_32) ** 2)
            a, b = product[:PAIRS], product[PAIRS:]
            real_part = a[:, :PAIRS] + b[:, PAIRS:]
            imag_part = a[:, PAIRS:] - b[:, :PAIRS]
            out_ref[top, :] = jnp.concatenate([real_part, imag_part], axis=1) * scale
            return carry

        lax.fori_loop(0, pairs, finish, 0)


def waves_spec(waves, last):
    shape = (waves.shape[0], STEP_Z) + waves.shape[2:]
    return pl.BlockSpec(shape, lambda i, who: (0, jnp.minimum(i, last), 0, 0, 0))


def all_responses(who, waves, inter):
    pairs = waves.shape[2]
    rows2 = inter.shape[2]
    half2 = 2 * pairs * PAIRS
    steps = NZ // STEP_Z
    spec = pltpu.PrefetchScalarGridSpec(
        num_scalar_prefetch=1,
        grid=(steps + 1,),
        in_specs=[
            waves_spec(waves, steps - 1),
            pl.BlockSpec((STEP_Z, NXY, rows2), lambda i, who: (jnp.maximum(i - 1, 0), 0, 0)),
        ],
        out_specs=pl.BlockSpec((half2, rows2), lambda i, who: (0, 0)),
        scratch_shapes=[pltpu.VMEM((half2, STEP_Z * NXY), BF)] * 2,
    )
    return pl.pallas_call(
        functools.partial(response_kernel, pairs),
        grid_spec=spec,
        out_shape=jax.ShapeDtypeStruct((half2, rows2), F32),
        compiler_params=pltpu.CompilerParams(vmem_limit_bytes=VMEM_LIMIT),
        cost_estimate=pl.CostEstimate(
            flops=2 * half2 * rows2 * NG, bytes_accessed=2 * inter.size, transcendentals=0
        ),
    )(who, waves, inter)


def partial_blocks(who, waves, response, first, second):
    pairs = waves.shape[2]
    half2, rows2 = response.shape
    spec = pltpu.PrefetchScalarGridSpec(
        num_scalar_prefetch=1,
        grid=(NZ // STEP_Z,),
        in_specs=[
            waves_spec(waves, NZ // STEP_Z - 1),
            pl.BlockSpec((half2, rows2), lambda i, who: (0, 0)),
            pl.BlockSpec(first.shape, lambda i, who: (0, 0)),
            pl.BlockSpec((1,) + second.shape[1:], lambda i, who: (i, 0, 0)),
        ],
        out_specs=pl.BlockSpec((pairs * PAIRS, 2 * PAIRS), lambda i, who: (0, 0)),
        scratch_shapes=[
            pltpu.VMEM((half2, STEP_Z * NXY), BF),
            pltpu.VMEM((half2, STEP_Z * NXY), BF),
            pltpu.VMEM((half2, rows2), F32),
        ],
    )
    return pl.pallas_call(
        functools.partial(block_kernel, pairs),
        grid_spec=spec,
        out_shape=jax.ShapeDtypeStruct((pairs * PAIRS, 2 * PAIRS), F32),
        compiler_params=pltpu.CompilerParams(vmem_limit_bytes=VMEM_LIMIT),
        cost_estimate=pl.CostEstimate(
            flops=half2 * rows2 * NG, bytes_accessed=4 * response.size, transcendentals=0
        ),
    )(who, waves, response, first, second)


def sum_kernel(
    holders, members, part_ref, out_ref, got_ref, all_ref, send1, recv1, send2, recv2, send3, recv3
):
    ka = lax.axis_index("ka")
    ga = lax.axis_index("ga")
    size = part_ref.shape[0] // members
    mesh_id = pl.DeviceIdType.MESH
    barrier = pltpu.get_barrier_semaphore()

    def member(d):
        return lax.rem(ga + d, members)

    def holder(e):
        return lax.rem(ka + e, holders)

    def block(place):
        return pl.ds(pl.multiple_of(place * size, size), size)

    def scatter(d):
        return pltpu.make_async_remote_copy(
            src_ref=part_ref.at[block(member(d))],
            dst_ref=got_ref.at[d],
            send_sem=send1.at[d],
            recv_sem=recv1.at[d],
            device_id=(ka, member(d)),
            device_id_type=mesh_id,
        )

    def gather(d):
        return pltpu.make_async_remote_copy(
            src_ref=all_ref.at[ka, block(ga)],
            dst_ref=all_ref.at[ka, block(ga)],
            send_sem=send2.at[d],
            recv_sem=recv2.at[d],
            device_id=(ka, member(d)),
            device_id_type=mesh_id,
        )

    def exchange(e):
        return pltpu.make_async_remote_copy(
            src_ref=all_ref.at[ka],
            dst_ref=all_ref.at[ka],
            send_sem=send3.at[e],
            recv_sem=recv3.at[e],
            device_id=(holder(e), ga),
            device_id_type=mesh_id,
        )

    def loop(count, body):
        def run(i, carry):
            body(i)
            return carry

        lax.fori_loop(1, count, run, 0)

    def greet(device):
        pl.semaphore_signal(barrier, inc=1, device_id=device, device_id_type=mesh_id)

    loop(members, lambda d: greet((ka, member(d))))
    loop(holders, lambda e: greet((holder(e), ga)))
    pl.semaphore_wait(barrier, members + holders - 2)

    loop(members, lambda d: scatter(d).start())
    all_ref[ka, block(ga), :] = part_ref[block(ga), :]

    def add(d):
        scatter(d).wait_recv()
        all_ref[ka, block(ga), :] += got_ref[d]

    loop(members, add)
    loop(members, lambda d: gather(d).start())
    loop(members, lambda d: gather(d).wait_recv())
    loop(holders, lambda e: exchange(e).start())
    loop(members, lambda d: scatter(d).wait_send())
    loop(members, lambda d: gather(d).wait_send())
    loop(holders, lambda e: exchange(e).wait())
    out_ref[...] = all_ref[...]


def summed_everywhere(part, holders, members):
    rows, lanes = part.shape
    size = rows // members
    return pl.pallas_call(
        functools.partial(sum_kernel, holders, members),
        out_shape=jax.ShapeDtypeStruct((holders, rows, lanes), F32),
        in_specs=[pl.BlockSpec(memory_space=pltpu.VMEM)],
        out_specs=pl.BlockSpec(memory_space=pltpu.VMEM),
        scratch_shapes=[
            pltpu.VMEM((members, size, lanes), F32),
            pltpu.VMEM((holders, rows, lanes), F32),
        ]
        + [pltpu.SemaphoreType.DMA((members,))] * 4
        + [pltpu.SemaphoreType.DMA((holders,))] * 2,
        compiler_params=pltpu.CompilerParams(
            collective_id=0, has_side_effects=True, vmem_limit_bytes=VMEM_LIMIT
        ),
    )(part)


def mirror_kernel(source_ref, blocks_ref, out_ref):
    del source_ref

    def swapped(size, axis):
        row = lax.broadcasted_iota(jnp.int32, (size, size), axis)
        column = lax.broadcasted_iota(jnp.int32, (size, size), 1 - axis)
        inner = row % PAIRS
        return (column == row - inner + (inner % 8) * 8 + inner // 8).astype(F32)

    highest = lax.Precision.HIGHEST
    left = jnp.dot(swapped(PAIRS, 0), blocks_ref[0], precision=highest)
    both = jnp.dot(left, swapped(2 * PAIRS, 1), precision=highest)
    lane = lax.broadcasted_iota(jnp.int32, both.shape, 1)
    out_ref[0] = jnp.where(lane < PAIRS, both, -both)


def mirrored(source, blocks):
    shape = (1,) + blocks.shape[1:]
    spec = pltpu.PrefetchScalarGridSpec(
        num_scalar_prefetch=1,
        grid=(source.shape[0],),
        in_specs=[pl.BlockSpec(shape, lambda i, source: (source[i], 0, 0))],
        out_specs=pl.BlockSpec(shape, lambda i, source: (i, 0, 0)),
    )
    return pl.pallas_call(
        mirror_kernel,
        grid_spec=spec,
        out_shape=jax.ShapeDtypeStruct((source.shape[0],) + blocks.shape[1:], F32),
    )(source, blocks)


def local_tables(gmap, place, rows):
    columns = rows // NZ
    number = place * columns + jnp.arange(columns, dtype=jnp.int32)
    gx, gy = number // NY, number % NY
    r = jnp.arange(NXY, dtype=jnp.int32)
    turns = ((r // NY)[:, None] * gx[None] + (r % NY)[:, None] * gy[None]) % NX
    angle = turns.astype(F32) * (-2.0 * math.pi / NX)
    plane = SCALE_16 * jnp.stack([jnp.cos(angle), jnp.sin(angle)], axis=1)
    same = jnp.asarray(np.eye(STEP_Z), F32)
    first = same[:, None, :, None, None] * plane[None, :, None]
    first = first.reshape(STEP_Z * NXY, STEP_Z * 2 * columns).astype(BF)
    gz = lax.dynamic_slice_in_dim(gmap, place * rows, rows) % NZ
    z = jnp.arange(NZ, dtype=jnp.int32)
    angle = (z[:, None] * gz[None] % NZ).astype(F32) * (-2.0 * math.pi / NZ)
    c, s = SCALE_32 * jnp.cos(angle), SCALE_32 * jnp.sin(angle)
    line = jnp.stack([jnp.stack([c, s], axis=1), jnp.stack([-s, c], axis=1)], axis=1)
    own = (jnp.arange(rows) // NZ)[None, :] == jnp.arange(columns)[:, None]
    second = jnp.where(own[None, None, :, None, :], line[:, :, None], 0.0)
    second = second.reshape(NZ // STEP_Z, STEP_Z * 2 * columns, 2 * rows).astype(BF)
    return first, second


def flattened(blocks):
    number = blocks.shape[0]
    parts = blocks.reshape(number, PAIRS, 2, PAIRS).transpose(0, 2, 1, 3)
    return parts.reshape(number, 2, PAIRS * PAIRS)


def on_device(holders, members, wavefunctions, partner, gmap, screened):
    pairs, _, _, planes, _ = wavefunctions.shape
    ka_place = lax.axis_index("ka")
    ga_place = lax.axis_index("ga")
    owned = ka_place * pairs + jnp.arange(pairs, dtype=jnp.int32)
    wanted = partner[owned]
    by_plane = wavefunctions.transpose(3, 0, 1, 2, 4)
    val = by_plane[:, :, :, :NV].reshape(planes, pairs, 2 * NV, NXY)
    cond = by_plane[:, :, :, NV:].reshape(planes, pairs, 2 * NC, NXY)
    inter, val, cond = transformed_interaction(holders, members, gmap, screened, val, cond)
    first, second = local_tables(gmap, ga_place, screened.shape[0])
    who = jnp.concatenate([ka_place[None].astype(jnp.int32), wanted // pairs, wanted % pairs])
    response = all_responses(who, val, inter)
    part = partial_blocks(who, cond, response, first, second)
    everyone = summed_everywhere(part, holders, members)
    everyone = everyone.reshape(holders * pairs, PAIRS, 2 * PAIRS)
    source = jnp.sum(
        jnp.where(
            partner[None, :] == owned[:, None],
            jnp.arange(partner.shape[0], dtype=jnp.int32)[None],
            0,
        ),
        axis=1,
    )
    own = lax.dynamic_slice_in_dim(everyone, ka_place * pairs, pairs)
    return (flattened(own), flattened(mirrored(source, everyone)))


def solution(mesh):
    in_specs = (P("ka", None, None, "ga", None), P(), P(), P("ga", None))
    out_specs = (P("ka", None, None), P("ka", None, None))
    return jax.shard_map(
        functools.partial(on_device, mesh.shape["ka"], mesh.shape["ga"]),
        mesh=mesh,
        in_specs=in_specs,
        out_specs=out_specs,
        check_vma=False,
    )
```
